32 devices in a mesh: seq: 16 (over z, y, x), head: 2 (over core).
Axes of the slice: x: 2, y: 2, z: 4, core: 2. Of those that a mesh axis runs over, the one named last changes fastest.
Arguments:
- layer_input: bfloat16 [2048, 4096], P('seq', 'head'), may hold values from -6 to 6
- query_rows: bfloat16 [2048, 2048], P('seq', 'head'), may hold values from -6 to 6
- key_matrix_rows: bfloat16 [2048, 2048], P('seq', 'head'), may hold values from -1.25 to 1.25
- value_rows: bfloat16 [2048, 2048], P('seq', 'head'), may hold values from -6 to 6
- beta_rows: float32 [2048, 16], P('seq', 'head'), may hold values from 0 to 0.9, as said below
- log_gate: float32 [2048, 16], P('seq', 'head'), may hold values from -1.3 to 0, as said below
- grad_out: bfloat16 [2048, 2048], P('seq', 'head'), may hold values from -6 to 6
Outputs:
- grad_query: bfloat16 [2048, 2048], P('seq', 'head')
- grad_key: bfloat16 [2048, 2048], P('seq', 'head')
- grad_value: bfloat16 [2048, 2048], P('seq', 'head')
- grad_beta: float32 [2048, 16], P('seq', 'head')
- grad_log_gate: float32 [2048, 16], P('seq', 'head')
- grad_weight: bfloat16 [4096, 2048], P(None, 'head')
The draws below stay inside these ranges and needn't reach their ends.
Inputs may be any that keep to these rules, and one draw needn't show every extreme that they name: `beta_rows`: write strengths vary from token to token and from head to head. `log_gate`: decay rates vary from token to token and from head to head.
All inputs are finite; a program needn't handle non-finite values.
Results may differ from the reference program's by a relative error of at most 0.0049.
Values may be sent and summed in bfloat16 or wider, within the bound.
No kernel may reach another device: no remote copies, remote signals or barrier semaphores. Data moves between devices by JAX's collectives and lax.ppermute only.
A program may use at most 128 MiB of HBM per device.

```python
import jax
import jax.numpy as jnp
from jax import lax

D = 4096
HEADS = 16
HD = 128
BLOCK = 64
TOK_DEV = 128
TOKENS = 2048


def head_kinds(key):
    picks = jax.random.randint(jax.random.fold_in(key, 11), (HEADS,), 0, 2)
    return picks.astype(jnp.float32)


def log_uniform(key, shape, lower_end, upper_end):
    return jnp.exp(jax.random.uniform(key, shape, jnp.float32, jnp.log(lower_end), jnp.log(upper_end)))


def draw_beta_rows(key, part):
    fast = head_kinds(key)
    fast_part = jax.random.uniform(jax.random.fold_in(key, 31), (TOKENS, HEADS), jnp.float32, 0.2, 0.9)
    slow_part = log_uniform(jax.random.fold_in(key, 32), (TOKENS, HEADS), 0.15 * HD / TOKENS, 0.45 * HD / TOKENS)
    return jnp.where(fast[None, :] > 0.5, fast_part, slow_part).astype(jnp.float32)


def draw_log_gate(key, part):
    fast = head_kinds(key)
    slow_rate = log_uniform(jax.random.fold_in(key, 21), (TOKENS, HEADS), 0.1 / TOKENS, 0.3 / TOKENS)
    fast_rate = log_uniform(jax.random.fold_in(key, 22), (TOKENS, HEADS), 1.0 / 50.0, 1.0 / 30.0)
    fading_velocity = jnp.where(fast[None, :] > 0.5, fast_rate, slow_rate)
    blocks = log_uniform(jax.random.fold_in(key, 23), (TOKENS // TOK_DEV, HEADS), 0.5, 2.0)
    fading_velocity = fading_velocity * jnp.repeat(blocks, TOK_DEV, axis=0)
    element_slots = jax.random.randint(jax.random.fold_in(key, 24), (2, HEADS), 0, TOKENS)
    fading_losses = jnp.log(jax.random.uniform(jax.random.fold_in(key, 25), (2, HEADS), jnp.float32, 0.55, 0.8))
    element_offsets = jnp.arange(TOKENS)[:, None, None]
    spike_clusters = jnp.where(element_offsets == element_slots[None], fading_losses[None], 0.0).sum(axis=1)
    return (spike_clusters - fading_velocity).astype(jnp.float32)


def raised(array, rng, source, target, shards_of, factor):
    owner, partner = [(jnp.arange(array.shape[position]) // (array.shape[position] // shards_of)).reshape([-1 if axis == position else 1 for axis in range(array.ndim)]) for position in (source, target)]
    chosen = jax.random.permutation(rng, shards_of)[partner]
    strong = (owner == chosen) | (owner == (partner + shards_of // 2) % shards_of)
    return jnp.where(strong, factor * array, array)


def steps_of(rng, dims, cuts, low, top_value):
    def one(dim, parts):
        heights = jax.random.uniform(jax.random.fold_in(jax.random.fold_in(rng, 6), dim), (parts,), jnp.float32, low / len(cuts), top_value / len(cuts))
        return jnp.repeat(jnp.exp(heights), dims[dim] // parts).reshape((-1,) + (1,) * (len(dims) - dim - 1))

    level = one(*cuts[0])
    for cut in cuts[1:]:
        level = level * one(*cut)
    return level


def noise(stream_key, dims, deviation, most, cuts=(), kind=jnp.bfloat16):
    factor_of = steps_of(stream_key, dims, cuts, -0.22, 0.18) if cuts else 1.0
    values = jax.random.normal(stream_key, dims, jnp.float32) * deviation * factor_of
    return jnp.minimum(jnp.maximum(values, -most), most).astype(kind)


def gaussian_with(key, extent, scale, reach, shards, heavy, kind=jnp.bfloat16):
    entries = scale * jax.random.normal(key, extent, jnp.float32)
    if shards:
        entries = entries * steps_of(key, extent, shards, -0.22, 0.18)
    return jnp.clip(raised(entries, jax.random.fold_in(key, 3), *heavy), -reach, reach).astype(kind)


def setup_inputs(seed: int = 0) -> dict:
    streams_of = jax.random.split(jax.random.key(seed), 8)
    layer_input = gaussian_with(streams_of[0], (TOKENS, D), 1.0, 6.0, ((0, 16), (1, 2)), (0, 1, 16, 2.0))
    query_rows = noise(streams_of[1], (TOKENS, HEADS * HD), 1.0, 6.0, ((0, 16), (1, 2)))
    key_matrix_rows = noise(streams_of[2], (TOKENS, HEADS * HD), 0.088, 1.25, ((0, 16), (1, 2)))
    value_rows = noise(streams_of[3], (TOKENS, HEADS * HD), 1.0, 6.0, ((0, 16), (1, 2)))
    beta_rows = draw_beta_rows(jax.random.fold_in(streams_of[7], 71), 0)
    log_gate = draw_log_gate(jax.random.fold_in(streams_of[7], 71), 0)
    grad_out = noise(streams_of[6], (TOKENS, HEADS * HD), 1.0, 6.0, ((0, 16), (1, 2)))
    return dict(layer_input=layer_input, query_rows=query_rows, key_matrix_rows=key_matrix_rows, value_rows=value_rows, beta_rows=beta_rows, log_gate=log_gate, grad_out=grad_out)


HIGHEST_PRECISION = lax.Precision.HIGHEST

def product(left_side, right_side):
    return jnp.matmul(left_side, right_side, precision=HIGHEST_PRECISION)

def flipped(matrix):
    return jnp.swapaxes(matrix, -1, -2)

def unit_inverse(strict_lower):
    order_size = strict_lower.shape[-1]
    identity = jnp.eye(order_size, dtype=strict_lower.dtype)
    result = identity - strict_lower
    exponent_summand = strict_lower
    covered = 2
    while covered < order_size:
        exponent_summand = product(exponent_summand, exponent_summand)
        result = product(result, identity + exponent_summand)
        covered = covered * 2
    return result

def block_parts(key_block, strength, log_decay):
    order_size = log_decay.shape[-1]
    running = jnp.cumsum(log_decay, axis=-1)
    line_number = lax.broadcasted_iota(jnp.int32, (order_size, order_size), 0)
    col_index = lax.broadcasted_iota(jnp.int32, (order_size, order_size), 1)
    causal = line_number >= col_index
    strict = line_number > col_index
    spread = running[..., :, None] - running[..., None, :]
    decay_table = jnp.where(causal, jnp.exp(jnp.where(causal, spread, 0.0)), 0.0)
    strict_lower = jnp.where(strict, strength[..., :, None] * decay_table * product(key_block, flipped(key_block)), 0.0)
    growth = jnp.exp(running)
    tail_decay = jnp.exp(running[..., -1:] - running)
    return (decay_table, growth, tail_decay, unit_inverse(strict_lower))

def segment(query_block, key_block, value_block, strength, log_decay, init_state, with_out):
    decay_table, growth, tail_decay, inverse = block_parts(key_block, strength, log_decay)
    pseudo = product(inverse, strength[..., None] * value_block)
    erasure = product(inverse, (strength * growth)[..., None] * key_block)
    written = flipped(tail_decay[..., None] * key_block)
    keep_all = growth[..., -1]
    argument_sequence = [pseudo, erasure, written, keep_all]
    if with_out:
        argument_sequence = argument_sequence + [decay_table * product(query_block, flipped(key_block)), growth[..., None] * query_block]

    def advance(carry_state, pieces):
        update = pieces[0] - product(pieces[1], carry_state)
        after_state = pieces[3] * carry_state + product(pieces[2], update)
        if with_out:
            return (after_state, product(pieces[5], carry_state) + product(pieces[4], update))
        return (after_state, None)
    return lax.scan(advance, init_state, tuple(argument_sequence))

def head_grads(pieces):
    query_head, key_head, value_head, strength_head, decay_head, grad_head = pieces
    block_count = TOKENS // BLOCK

    def forward(query_all, key_all, value_all, strength_all, decay_all):
        zero_state = jnp.zeros((HD, HD), jnp.float32)
        final_state, outputs = segment(query_all.reshape(block_count, BLOCK, HD), key_all.reshape(block_count, BLOCK, HD), value_all.reshape(block_count, BLOCK, HD), strength_all.reshape(block_count, BLOCK), decay_all.reshape(block_count, BLOCK), zero_state, True)
        return outputs.reshape(TOKENS, HD)
    outputs, pull_back = jax.vjp(forward, query_head.astype(jnp.float32), key_head.astype(jnp.float32), value_head.astype(jnp.float32), strength_head, decay_head)
    return pull_back(grad_head.astype(jnp.float32))

def reference(layer_input, query_rows, key_matrix_rows, value_rows, beta_rows, log_gate, grad_out):

    def per_head_apply(matrix):
        return matrix.reshape(TOKENS, HEADS, HD).transpose(1, 0, 2)

    def to_rows(tensor):
        return tensor.transpose(1, 0, 2).reshape(TOKENS, HEADS * HD).astype(jnp.bfloat16)
    gradients = lax.map(head_grads, (per_head_apply(query_rows), per_head_apply(key_matrix_rows), per_head_apply(value_rows), beta_rows.T, log_gate.T, per_head_apply(grad_out)))
    grad_value = to_rows(gradients[2])
    grad_weight = jnp.dot(layer_input.T, grad_value, preferred_element_type=jnp.float32).astype(jnp.bfloat16)
    return (to_rows(gradients[0]), to_rows(gradients[1]), grad_value, gradients[3].T, gradients[4].T, grad_weight)
```

```python
from functools import partial

import jax
import jax.numpy as jnp
from jax import lax
from jax.experimental import pallas as pl
from jax.experimental.pallas import tpu as pltpu
from jax.sharding import PartitionSpec as P

f32 = jnp.float32
bf16 = jnp.bfloat16
PAD = 16
VMEM_LIMIT = 48 * 1024 * 1024

NN = (((1,), (0,)), ((), ()))
NT = (((1,), (1,)), ((), ()))
TN = (((0,), (0,)), ((), ()))


def dot(a, b, dims):
    return lax.dot_general(a, b, dims, preferred_element_type=f32)


def split(x):
    hi = x.astype(bf16)
    return hi, (x - hi.astype(f32)).astype(bf16)


def join(parts, axis):
    return jnp.concatenate(parts, axis=axis)


def mm(a, b, dims):
    (ca,), (cb,) = dims[0]
    if isinstance(a, tuple) and isinstance(b, tuple):
        return dot(join([a[0], a[1]], ca), join([b[0], b[0]], cb), dims) + dot(a[0], b[1], dims)
    if isinstance(a, tuple):
        return dot(join([a[0], a[1]], ca), join([b, b], cb), dims)
    if isinstance(b, tuple):
        return dot(join([a, a], ca), join([b[0], b[1]], cb), dims)
    return dot(a, b, dims)


def thirds(x):
    one = x.astype(bf16)
    rest = x - one.astype(f32)
    two = rest.astype(bf16)
    return one, two, (rest - two.astype(f32)).astype(bf16)


def pack_scalars(first, second):
    pieces = [p.astype(f32) for p in thirds(first) + thirds(second)]
    rows, width = first.shape
    out = []
    for r in range(rows):
        lines = [p[r : r + 1] for p in pieces] + [jnp.zeros((PAD - 6, width), f32)]
        out.append(jnp.concatenate(lines, axis=0).astype(bf16))
    return out


def unpack_scalars(tile):
    t = tile.astype(f32)
    return t[0:1] + t[1:2] + t[2:3], t[3:4] + t[4:5] + t[5:6]


def iotas(size):
    return (
        lax.broadcasted_iota(jnp.int32, (size, size), 0),
        lax.broadcasted_iota(jnp.int32, (size, size), 1),
    )


def turn_kernel(x_ref, out_ref):
    out_ref[...] = jnp.transpose(x_ref[...])


def pack_kernel(q_ref, k_ref, v_ref, g_ref, beta_ref, gate_ref, out_ref):
    length, heads = beta_ref.shape
    width = q_ref.shape[1] // heads
    scalars = pack_scalars(jnp.transpose(beta_ref[...]), jnp.transpose(gate_ref[...]))
    for h in range(heads):
        for place, ref in enumerate((q_ref, k_ref, v_ref, g_ref)):
            out_ref[h, pl.ds(place * length, length), :] = ref[:, pl.ds(h * width, width)]
        out_ref[h, pl.ds(4 * length, PAD), :] = scalars[h]


def scalars_of(slab_ref, count, length):
    betas, gates = [], []
    for c in range(count):
        b, g = unpack_scalars(slab_ref[c, pl.ds(4 * length, PAD), :])
        betas.append(b)
        gates.append(g)
    beta = jnp.concatenate(betas, axis=0)
    gate = jnp.concatenate(gates, axis=0)
    line, col = iotas(length)
    upper = (line <= col).astype(f32)
    running = lax.dot_general(
        gate, upper, NN, precision=lax.Precision.HIGHEST, preferred_element_type=f32
    )
    return running, jnp.transpose(running), jnp.transpose(beta)


def decay_of(run_col, run_row, causal):
    return jnp.where(causal, jnp.exp(jnp.where(causal, run_col - run_row, 0.0)), 0.0)


def first_kernel(slab_ref, maps_ref, aux_ref, ends_ref, inv_ref, low_ref):
    count = slab_ref.shape[0]
    width = slab_ref.shape[2]
    length = (slab_ref.shape[1] - PAD) // 4
    running, run_cols, beta_cols = scalars_of(slab_ref, count, length)
    line, col = iotas(length)
    causal = line >= col
    strict = line > col
    eye = (line == col).astype(f32)

    def part(c, place):
        return slab_ref[c, pl.ds(place * length, length), :]

    for c in range(count):
        decay = decay_of(run_cols[:, c : c + 1], running[c : c + 1, :], causal)
        k = part(c, 1)
        low = jnp.where(strict, beta_cols[:, c : c + 1] * decay * dot(k, k, NT), 0.0)
        low_ref[c] = low
        inv_ref[c] = eye - jnp.where((line ^ col) == 1, low, 0.0)
    size = 2
    while size < length:
        mask = ((line // size) ^ (col // size)) == 1
        for c in range(count):
            inv = split(inv_ref[c])
            side = split(jnp.where(mask, low_ref[c], 0.0))
            mid = split(mm(side, inv, NN))
            inv_ref[c] = inv_ref[c] - mm(inv, mid, NN)
        size = size * 2

    for c in range(count):
        run_col = run_cols[:, c : c + 1]
        beta = beta_cols[:, c : c + 1]
        grow = jnp.exp(run_col)
        last = running[c : c + 1, length - 1 : length]
        tail = jnp.exp(last - run_col)
        decay = decay_of(run_col, running[c : c + 1, :], causal)
        q, k, v, g = (part(c, i) for i in range(4))
        qf, kf, vf, gf = (a.astype(f32) for a in (q, k, v, g))
        inv = split(inv_ref[c])
        pairs = split(decay * dot(q, k, NT))
        both = mm(inv, split(join([(beta * grow) * kf, beta * vf], 1)), NN)
        aux_ref[c, 0] = both[:, :width]
        aux_ref[c, 1] = both[:, width:]
        moved = mm(k, split(tail * both), TN)
        eye_d = (
            lax.broadcasted_iota(jnp.int32, (width, width), 0)
            == lax.broadcasted_iota(jnp.int32, (width, width), 1)
        ).astype(f32)
        maps_ref[c, 0] = jnp.exp(last) * eye_d - moved[:, :width]
        maps_ref[c, 1] = moved[:, width:]
        back = mm(inv, split(join([mm(pairs, g, TN), tail * kf], 1)), TN)
        aux_ref[c, 2] = back[:, :width]
        aux_ref[c, 3] = back[:, width:]
        maps_ref[c, 2] = mm(g, split(grow * qf), TN) - mm(split((beta * grow) * back[:, :width]), k, TN)

    state = maps_ref[0, 1]
    adjoint = maps_ref[count - 1, 2]
    total = maps_ref[0, 0]
    for c in range(1, count):
        trans = split(maps_ref[c, 0])
        state = mm(trans, split(state), NN) + maps_ref[c, 1]
        total = mm(trans, split(total), NN)
        r = count - 1 - c
        adjoint = mm(split(adjoint), split(maps_ref[r, 0]), NN) + maps_ref[r, 2]
    ends_ref[0] = state
    ends_ref[1] = adjoint
    ends_ref[2] = total


def second_kernel(slab_ref, maps_ref, aux_ref, start_ref, finish_ref, dv_ref, out_ref, state_ref, adj_ref):
    count = slab_ref.shape[0]
    width = slab_ref.shape[2]
    length = (slab_ref.shape[1] - PAD) // 4
    running, run_cols, beta_cols = scalars_of(slab_ref, count, length)
    line, col = iotas(length)
    causal = line >= col
    strict = line > col

    state_ref[0] = start_ref[...]
    adj_ref[count - 1] = finish_ref[...]
    for c in range(1, count):
        state_ref[c] = mm(split(maps_ref[c - 1, 0]), split(state_ref[c - 1]), NN) + maps_ref[c - 1, 1]
        r = count - 1 - c
        adj_ref[r] = mm(split(adj_ref[r + 1]), split(maps_ref[r + 1, 0]), NN) + maps_ref[r + 1, 2]

    grad_beta, grad_run, consts = [], [], []
    for c in range(count):
        run_col = run_cols[:, c : c + 1]
        beta = beta_cols[:, c : c + 1]
        grow = jnp.exp(run_col)
        last = running[c : c + 1, length - 1 : length]
        tail = jnp.exp(last - run_col)
        decay = decay_of(run_col, running[c : c + 1, :], causal)
        q, k, v, g = (slab_ref[c, pl.ds(i * length, length), :] for i in range(4))
        qf, kf, vf = (a.astype(f32) for a in (q, k, v))
        state = state_ref[c]
        adj = adj_ref[c]
        state_s, adj_s = split(state), split(adj)
        update = aux_ref[c, 1] - mm(split(aux_ref[c, 0]), state_s, NN)
        update_s = split(update)
        d_rhs = aux_ref[c, 2] + mm(split(aux_ref[c, 3]), adj_s, NT)
        d_rhs_s = split(d_rhs)
        d_pair = decay * mm(g, update_s, NT)
        d_low = jnp.where(strict, -decay * mm(d_rhs_s, update_s, NT), 0.0)
        dq = grow * mm(g, state_s, NT) + mm(split(d_pair), k, NN)
        row = mm(split(d_low), k, NN) - grow * mm(d_rhs_s, state_s, NT)
        dk_row = beta * row
        wrote = tail * mm(update_s, adj_s, NN)
        dk_col = wrote + mm(split(join([d_pair, beta * d_low], 0)), join([q, k], 0), TN)
        dv_ref[c] = (beta * d_rhs).astype(bf16)
        out_ref[c, pl.ds(0, length), :] = dq.astype(bf16)
        out_ref[c, pl.ds(length, length), :] = (dk_row + dk_col).astype(bf16)
        grad_beta.append(jnp.sum(d_rhs * vf + kf * row, axis=1, keepdims=True))
        grad_run.append(jnp.sum(qf * dq + kf * (dk_row - dk_col), axis=1, keepdims=True))
        carry = jnp.exp(last) * jnp.sum(state * jnp.transpose(adj)) + jnp.sum(kf * wrote)
        consts.append(carry)
    db = jnp.concatenate(grad_beta, axis=1)
    dr = jnp.concatenate(grad_run, axis=1)
    upper = (line <= col).astype(f32)
    dg = lax.dot_general(
        upper, dr, NN, precision=lax.Precision.HIGHEST, preferred_element_type=f32
    ) + jnp.concatenate(consts, axis=1)
    packed = pack_scalars(jnp.transpose(db), jnp.transpose(dg))
    for c in range(count):
        out_ref[c, pl.ds(2 * length, PAD), :] = packed[c]


def swap(x, mask):
    return lax.ppermute(x, "seq", [(i, i ^ mask) for i in range(lax.axis_size("seq"))])


def gather_parts(x):
    half = x.shape[0] // 2
    out = []
    far = [(m, swap(x, m) if m else x) for m in range(0, lax.axis_size("seq"), 4)]
    for m, own in far:
        side, down = swap(own, 1), swap(own, 2)
        out += [(m, 0, own), (m | 1, 0, side), (m | 2, 0, down)]
        out += [(m | 3, 0, swap(down[:half], 1)), (m | 3, half, swap(side[half:], 2))]
    return out


def place_kernel(where, place_ref, *refs):
    parts, (all_ref, rows_ref) = refs[: len(where)], refs[len(where) :]
    shards, count, length, width = all_ref.shape
    heads = rows_ref.shape[1] // width
    me = place_ref[0]
    for (mask, first), part in zip(where, parts):
        all_ref[me ^ mask, pl.ds(first, part.shape[0])] = part[...]
    group = me // heads * heads
    for h in range(heads):
        rows_ref[:, pl.ds(h * width, width)] = all_ref[group + h, me - group]


def unpack_kernel(back_ref, dq_ref, dk_ref, dbeta_ref, dgate_ref):
    heads = back_ref.shape[0]
    length, width = dq_ref.shape[0], dq_ref.shape[1] // heads
    betas, gates = [], []
    for h in range(heads):
        lanes = pl.ds(h * width, width)
        dq_ref[:, lanes] = back_ref[h, pl.ds(0, length), :]
        dk_ref[:, lanes] = back_ref[h, pl.ds(length, length), :]
        b, g = unpack_scalars(back_ref[h, pl.ds(2 * length, PAD), :])
        betas.append(b)
        gates.append(g)
    dbeta_ref[...] = jnp.transpose(jnp.concatenate(betas, axis=0))
    dgate_ref[...] = jnp.transpose(jnp.concatenate(gates, axis=0))


def weight_kernel(x_ref, dv_ref, out_ref):
    shards = x_ref.shape[0]
    groups, heads, count = dv_ref.shape[:3]
    total = None
    step = 2 if count % 2 == 0 else 1
    for s in range(0, shards, step):
        left = join([x_ref[s + i, 0] for i in range(step)], 1)
        right = join(
            [join([dv_ref[(s + i) // count, h, (s + i) % count] for h in range(heads)], 1) for i in range(step)], 0
        )
        term = dot(left, right, NN)
        total = term if total is None else total + term
    out_ref[...] = total.astype(out_ref.dtype)


def weight_grad(x_all, dv_all, block):
    shards, halves, feats, length = x_all.shape
    groups, heads, count, _, width = dv_all.shape
    per = feats // block
    return pl.pallas_call(
        weight_kernel,
        grid=(halves * per,),
        in_specs=[
            pl.BlockSpec((shards, 1, block, length), lambda i: (0, i // per, i % per, 0)),
            pl.BlockSpec(dv_all.shape, lambda i: (0, 0, 0, 0, 0)),
        ],
        out_specs=pl.BlockSpec((block, heads * width), lambda i: (i, 0)),
        out_shape=jax.ShapeDtypeStruct((halves * feats, heads * width), bf16),
        compiler_params=pltpu.CompilerParams(vmem_limit_bytes=VMEM_LIMIT),
    )(x_all, dv_all)


def whole_call(kernel, outs, scratch=(), flops=0):
    return pl.pallas_call(
        kernel,
        out_shape=[jax.ShapeDtypeStruct(s, d) for s, d in outs],
        scratch_shapes=[pltpu.VMEM(s, d) for s, d in scratch],
        compiler_params=pltpu.CompilerParams(vmem_limit_bytes=VMEM_LIMIT),
    )


def shards(layer_input, query_rows, key_matrix_rows, value_rows, beta_rows, log_gate, grad_out):
    length, heads = beta_rows.shape
    width = query_rows.shape[1] // heads
    seq = lax.axis_size("seq")
    halves = lax.axis_size("head")
    groups = seq // heads
    count = heads
    members = [[g * heads + i for i in range(heads)] for g in range(groups)]

    slabs = whole_call(pack_kernel, [((heads, 4 * length + PAD, width), bf16)])(
        query_rows, key_matrix_rows, value_rows, grad_out, beta_rows, log_gate
    )[0]
    slabs = lax.all_to_all(slabs, "seq", 0, 0, axis_index_groups=members, tiled=True)
    turned = whole_call(turn_kernel, [(layer_input.shape[::-1], bf16)])(layer_input)[0]
    x_all = lax.all_gather(turned, ("seq", "head"), axis=0).reshape(
        (seq, halves) + turned.shape
    )

    square = (width, width)
    maps, aux, ends = whole_call(
        first_kernel,
        [((count, 3) + square, f32), ((count, 4, length, width), f32), ((3,) + square, f32)],
        [((count, length, length), f32), ((count, length, length), f32)],
    )(slabs)
    up = [(s, s + heads) for s in range(seq - heads)]
    down = [(s + heads, s) for s in range(seq - heads)]
    start = lax.ppermute(ends[0], "seq", up)
    finish = lax.ppermute(ends[1], "seq", down)
    for _ in range(groups - 2):
        start = lax.ppermute(
            jnp.matmul(ends[2], start, precision=lax.Precision.HIGHEST) + ends[0], "seq", up
        )
        finish = lax.ppermute(
            jnp.matmul(finish, ends[2], precision=lax.Precision.HIGHEST) + ends[1], "seq", down
        )

    dv, grads = whole_call(
        second_kernel,
        [((count, length, width), bf16), ((count, 2 * length + PAD, width), bf16)],
        [((count,) + square, f32), ((count,) + square, f32)],
    )(slabs, maps, aux, start, finish)
    back = lax.all_to_all(grads, "seq", 0, 0, axis_index_groups=members, tiled=True)

    rows = (length, heads * width)
    parts = gather_parts(dv)
    me = lax.axis_index("seq").astype(jnp.int32).reshape(1)
    vmem = pl.BlockSpec(memory_space=pltpu.VMEM)
    dv_all, dvo = pl.pallas_call(
        partial(place_kernel, [p[:2] for p in parts]),
        in_specs=[pl.BlockSpec(memory_space=pltpu.SMEM)] + [vmem] * len(parts),
        out_specs=[vmem, vmem],
        out_shape=[
            jax.ShapeDtypeStruct((seq, count, length, width), bf16),
            jax.ShapeDtypeStruct(rows, bf16),
        ],
        compiler_params=pltpu.CompilerParams(vmem_limit_bytes=VMEM_LIMIT),
    )(me, *[p[2] for p in parts])
    dv_all = dv_all.reshape(groups, heads, count, length, width)
    dq, dk, dbeta, dgate = whole_call(
        unpack_kernel, [(rows, bf16), (rows, bf16), ((length, heads), f32), ((length, heads), f32)]
    )(back)
    weight = weight_grad(x_all, dv_all, min(512, layer_input.shape[1]))
    return dq, dk, dvo, dbeta, dgate, weight


def solution(mesh):
    row = P("seq", "head")
    return jax.shard_map(
        shards, mesh=mesh, in_specs=(row,) * 7, out_specs=(row,) * 5 + (P(None, "head"),), check_vma=False
    )
```

```python
from functools import partial

import jax
import jax.numpy as jnp
from jax import lax
from jax.experimental import pallas as pl
from jax.experimental.pallas import tpu as pltpu
from jax.sharding import PartitionSpec as P

f32 = jnp.float32
bf16 = jnp.bfloat16
PAD = 16
PLAIN = 0
VMEM_MOST = 60 * 1024 * 1024
VMEM_LIMIT = 48 * 1024 * 1024

NN = (((1,), (0,)), ((), ()))
NT = (((1,), (1,)), ((), ()))
TN = (((0,), (0,)), ((), ()))


def dot(a, b, dims):
    return lax.dot_general(a, b, dims, preferred_element_type=f32)


def split(x):
    hi = x.astype(bf16)
    return hi, (x - hi.astype(f32)).astype(bf16)


def join(parts, axis):
    return jnp.concatenate(parts, axis=axis)


def mm(a, b, dims):
    (ca,), (cb,) = dims[0]
    if isinstance(a, tuple) and isinstance(b, tuple):
        return dot(join([a[0], a[1]], ca), join([b[0], b[0]], cb), dims) + dot(a[0], b[1], dims)
    if isinstance(a, tuple):
        return dot(join([a[0], a[1]], ca), join([b, b], cb), dims)
    if isinstance(b, tuple):
        return dot(join([a, a], ca), join([b[0], b[1]], cb), dims)
    return dot(a, b, dims)


def thirds(x):
    one = x.astype(bf16)
    rest = x - one.astype(f32)
    two = rest.astype(bf16)
    return one, two, (rest - two.astype(f32)).astype(bf16)


def pack_scalars(first, second):
    pieces = [p.astype(f32) for p in thirds(first) + thirds(second)]
    rows, width = first.shape
    out = []
    for r in range(rows):
        lines = [p[r : r + 1] for p in pieces] + [jnp.zeros((PAD - 6, width), f32)]
        out.append(jnp.concatenate(lines, axis=0).astype(bf16))
    return out


def unpack_scalars(tile):
    t = tile.astype(f32)
    return t[0:1] + t[1:2] + t[2:3], t[3:4] + t[4:5] + t[5:6]


def iotas(size):
    return (
        lax.broadcasted_iota(jnp.int32, (size, size), 0),
        lax.broadcasted_iota(jnp.int32, (size, size), 1),
    )


def turn_kernel(x_ref, *out_refs):
    first = 0
    for out_ref in out_refs:
        here = out_ref.shape[0]
        out_ref[...] = jnp.transpose(x_ref[:, pl.ds(first, here)])
        first += here


def pack_kernel(q_ref, k_ref, v_ref, g_ref, beta_ref, gate_ref, out_ref, sems):
    heads, length = beta_ref.shape
    width = q_ref.shape[1] // heads
    copies = []
    for h in range(heads):
        for place, ref in enumerate((q_ref, k_ref, v_ref, g_ref)):
            copies.append(
                pltpu.make_async_copy(
                    ref.at[:, pl.ds(h * width, width)],
                    out_ref.at[h, pl.ds(place * length, length), :],
                    sems.at[h, place],
                )
            )
            copies[-1].start()
    for h, lines in enumerate(pack_scalars(beta_ref[...], gate_ref[...])):
        out_ref[h, pl.ds(4 * length, PAD), :] = lines
    for copy in copies:
        copy.wait()


def pack(arrays, beta, gate):
    heads, length = beta.shape
    width = arrays[0].shape[1] // heads
    return pl.pallas_call(
        pack_kernel,
        in_specs=[pl.BlockSpec(memory_space=pl.ANY)] * 4 + [pl.BlockSpec(memory_space=pltpu.VMEM)] * 2,
        out_specs=pl.BlockSpec(memory_space=pltpu.VMEM),
        out_shape=jax.ShapeDtypeStruct((heads, 4 * length + PAD, width), bf16),
        scratch_shapes=[pltpu.SemaphoreType.DMA((heads, 4))],
        compiler_params=pltpu.CompilerParams(vmem_limit_bytes=VMEM_MOST),
    )(*arrays, beta, gate)


def scalars_of(slab_ref, count, length):
    betas, gates = [], []
    for c in range(count):
        b, g = unpack_scalars(slab_ref[c, pl.ds(4 * length, PAD), :])
        betas.append(b)
        gates.append(g)
    beta = jnp.concatenate(betas, axis=0)
    gate = jnp.concatenate(gates, axis=0)
    line, col = iotas(length)
    upper = (line <= col).astype(f32)
    running = lax.dot_general(
        gate, upper, NN, precision=lax.Precision.HIGHEST, preferred_element_type=f32
    )
    return running, jnp.transpose(running), jnp.transpose(beta)


def decay_of(run_col, run_row, causal):
    return jnp.where(causal, jnp.exp(jnp.where(causal, run_col - run_row, 0.0)), 0.0)


def first_kernel(place_ref, slab_ref, maps_ref, aux_ref, ends_ref, inv_ref, low_ref):
    count = slab_ref.shape[0]
    width = slab_ref.shape[2]
    length = (slab_ref.shape[1] - PAD) // 4
    running, run_cols, beta_cols = scalars_of(slab_ref, count, length)
    line, col = iotas(length)
    causal = line >= col
    strict = line > col
    eye = (line == col).astype(f32)

    def part(c, place):
        return slab_ref[c, pl.ds(place * length, length), :]

    for c in range(count):
        decay = decay_of(run_cols[:, c : c + 1], running[c : c + 1, :], causal)
        k = part(c, 1)
        low = jnp.where(strict, beta_cols[:, c : c + 1] * decay * dot(k, k, NT), 0.0)
        low_ref[c] = low
        inv_ref[c] = eye - jnp.where((line ^ col) == 1, low, 0.0)
    size = 2
    while size < length:
        mask = ((line // size) ^ (col // size)) == 1
        for c in range(count):
            inv = split(inv_ref[c])
            side = split(jnp.where(mask, low_ref[c], 0.0))
            mid = split(mm(side, inv, NN))
            inv_ref[c] = inv_ref[c] - mm(inv, mid, NN)
        size = size * 2

    for c in range(count):
        run_col = run_cols[:, c : c + 1]
        beta = beta_cols[:, c : c + 1]
        grow = jnp.exp(run_col)
        last = running[c : c + 1, length - 1 : length]
        tail = jnp.exp(last - run_col)
        decay = decay_of(run_col, running[c : c + 1, :], causal)
        q, k, v, g = (part(c, i) for i in range(4))
        qf, kf, vf, gf = (a.astype(f32) for a in (q, k, v, g))
        inv = split(inv_ref[c])
        pairs = split(decay * dot(q, k, NT))
        both = mm(inv, split(join([(beta * grow) * kf, beta * vf], 1)), NN)
        aux_ref[c, 0] = both[:, :width]
        aux_ref[c, 1] = both[:, width:]
        moved = mm(k, split(tail * both), TN)
        eye_d = (
            lax.broadcasted_iota(jnp.int32, (width, width), 0)
            == lax.broadcasted_iota(jnp.int32, (width, width), 1)
        ).astype(f32)
        maps_ref[c, 0] = jnp.exp(last) * eye_d - moved[:, :width]
        maps_ref[c, 1] = moved[:, width:]
        back = mm(inv, split(join([mm(pairs, g, TN), tail * kf], 1)), TN)
        aux_ref[c, 2] = back[:, :width]
        aux_ref[c, 3] = back[:, width:]
        maps_ref[c, 2] = mm(g, split(grow * qf), TN) - mm(split((beta * grow) * back[:, :width]), k, TN)

    state = maps_ref[0, 1]
    adjoint = maps_ref[count - 1, 2]
    total = maps_ref[0, 0]
    for c in range(1, count):
        trans = split(maps_ref[c, 0])
        state = mm(trans, split(state), NN) + maps_ref[c, 1]
        total = mm(trans, split(total), NN)
        r = count - 1 - c
        adjoint = mm(split(adjoint), split(maps_ref[r, 0]), NN) + maps_ref[r, 2]
    ends_ref[0] = state
    ends_ref[1] = adjoint
    ends_ref[2] = total
    ends_ref[3] = jnp.where(place_ref[0] == 0, state, adjoint)


def second_kernel(place_ref, slab_ref, maps_ref, aux_ref, start_ref, finish_ref, dv_ref, out_ref, state_ref, adj_ref):
    count = slab_ref.shape[0]
    width = slab_ref.shape[2]
    length = (slab_ref.shape[1] - PAD) // 4
    running, run_cols, beta_cols = scalars_of(slab_ref, count, length)
    line, col = iotas(length)
    causal = line >= col
    strict = line > col

    state_ref[0] = jnp.where(place_ref[0] == 0, 0.0, start_ref[...])
    adj_ref[count - 1] = jnp.where(place_ref[0] == place_ref[1] - 1, 0.0, finish_ref[...])
    for c in range(1, count):
        state_ref[c] = mm(split(maps_ref[c - 1, 0]), split(state_ref[c - 1]), NN) + maps_ref[c - 1, 1]
        r = count - 1 - c
        adj_ref[r] = mm(split(adj_ref[r + 1]), split(maps_ref[r + 1, 0]), NN) + maps_ref[r + 1, 2]

    grad_beta, grad_run, consts = [], [], []
    for c in range(count):
        run_col = run_cols[:, c : c + 1]
        beta = beta_cols[:, c : c + 1]
        grow = jnp.exp(run_col)
        last = running[c : c + 1, length - 1 : length]
        tail = jnp.exp(last - run_col)
        decay = decay_of(run_col, running[c : c + 1, :], causal)
        q, k, v, g = (slab_ref[c, pl.ds(i * length, length), :] for i in range(4))
        qf, kf, vf = (a.astype(f32) for a in (q, k, v))
        state = state_ref[c]
        adj = adj_ref[c]
        state_s, adj_s = split(state), split(adj)
        update = aux_ref[c, 1] - mm(split(aux_ref[c, 0]), state_s, NN)
        update_s = split(update)
        d_rhs = aux_ref[c, 2] + mm(split(aux_ref[c, 3]), adj_s, NT)
        d_rhs_s = split(d_rhs)
        d_pair = decay * mm(g, update_s, NT)
        d_low = jnp.where(strict, -decay * mm(d_rhs_s, update_s, NT), 0.0)
        dq = grow * mm(g, state_s, NT) + mm(split(d_pair), k, NN)
        row = mm(split(d_low), k, NN) - grow * mm(d_rhs_s, state_s, NT)
        dk_row = beta * row
        wrote = tail * mm(update_s, adj_s, NN)
        dk_col = wrote + mm(split(join([d_pair, beta * d_low], 0)), join([q, k], 0), TN)
        dv_ref[c] = (beta * d_rhs).astype(bf16)
        out_ref[c, pl.ds(0, length), :] = dq.astype(bf16)
        out_ref[c, pl.ds(length, length), :] = (dk_row + dk_col).astype(bf16)
        grad_beta.append(jnp.sum(d_rhs * vf + kf * row, axis=1, keepdims=True))
        grad_run.append(jnp.sum(qf * dq + kf * (dk_row - dk_col), axis=1, keepdims=True))
        carry = jnp.exp(last) * jnp.sum(state * jnp.transpose(adj)) + jnp.sum(kf * wrote)
        consts.append(carry)
    db = jnp.concatenate(grad_beta, axis=1)
    dr = jnp.concatenate(grad_run, axis=1)
    upper = (line <= col).astype(f32)
    dg = lax.dot_general(
        upper, dr, NN, precision=lax.Precision.HIGHEST, preferred_element_type=f32
    ) + jnp.concatenate(consts, axis=1)
    packed = pack_scalars(jnp.transpose(db), jnp.transpose(dg))
    for c in range(count):
        out_ref[c, pl.ds(2 * length, PAD), :] = packed[c]


def swap(x, mask):
    return lax.ppermute(x, "seq", [(i, i ^ mask) for i in range(lax.axis_size("seq"))])


def corner(got, m):
    got[m | 3] = swap(got[m | 2], 1) if m == 12 else swap(got[m | 1], 2)


def sides(got, m):
    if m == 4:
        got[5], got[6] = swap(got[1], 4), swap(got[2], 4)
    else:
        got[m | 1], got[m | 2] = swap(got[m], 1), swap(got[m], 2)


def after(got, masks, *others):
    some = {m: got[m] for m in masks}
    return {**got, **lax.optimization_barrier((some,) + others)[0]}


def tied(x, got, masks):
    x, some = lax.optimization_barrier((x, {m: got[m] for m in masks if m in got}))
    return x, {**got, **some}


def stack_kernel(me_ref, *refs):
    parts, out_ref, sems = refs[:-2], refs[-2], refs[-1]
    copies = []
    for mask, part in enumerate(parts):
        copies.append(pltpu.make_async_copy(part, out_ref.at[me_ref[0] ^ mask], sems.at[mask]))
        copies[-1].start()
    for copy in copies:
        copy.wait()


def place_kernel(masks, all_heads, me_ref, *refs):
    parts, all_ref, sems = refs[:-2], refs[-2], refs[-1]
    width = parts[0].shape[2]
    heads = all_ref.shape[3] // width
    copies = []
    for i, (mask, part) in enumerate(zip(masks, parts)):
        source = me_ref[0] ^ mask
        lanes = pl.ds(pl.multiple_of(source % heads * width, width), width)
        copies.append(pltpu.make_async_copy(part, all_ref.at[source // all_heads, :, :, lanes], sems.at[i]))
        copies[-1].start()
    for copy in copies:
        copy.wait()


def rows_kernel(me_ref, *refs):
    parts, rows_ref, sems = refs[:-2], refs[-2], refs[-1]
    heads, width = len(parts), parts[0].shape[2]
    me = me_ref[0]
    copies = []
    for mask, part in enumerate(parts):
        lanes = pl.ds(pl.multiple_of((me ^ mask) % heads * width, width), width)
        copies.append(pltpu.make_async_copy(part.at[me % heads], rows_ref.at[:, lanes], sems.at[mask]))
        copies[-1].start()
    for copy in copies:
        copy.wait()


def arranged(kernel, got, me, outs):
    parts = [got[m] for m in sorted(got)]
    vmem = pl.BlockSpec(memory_space=pltpu.VMEM)
    return pl.pallas_call(
        kernel,
        in_specs=[pl.BlockSpec(memory_space=pltpu.SMEM)] + [pl.BlockSpec(memory_space=pl.ANY)] * len(parts),
        out_specs=[vmem] * len(outs),
        out_shape=[jax.ShapeDtypeStruct(o, bf16) for o in outs],
        scratch_shapes=[pltpu.SemaphoreType.DMA((len(parts),))],
        compiler_params=pltpu.CompilerParams(vmem_limit_bytes=VMEM_LIMIT),
    )(me.reshape(1), *parts)


def unpack_kernel(back_ref, dq_ref, dk_ref, dbeta_ref, dgate_ref):
    heads = back_ref.shape[0]
    length, width = dq_ref.shape[0], dq_ref.shape[1] // heads
    betas, gates = [], []
    for h in range(heads):
        lanes = pl.ds(h * width, width)
        dq_ref[:, lanes] = back_ref[h, pl.ds(0, length), :]
        dk_ref[:, lanes] = back_ref[h, pl.ds(length, length), :]
        b, g = unpack_scalars(back_ref[h, pl.ds(2 * length, PAD), :])
        betas.append(b)
        gates.append(g)
    dbeta_ref[...] = jnp.concatenate(betas, axis=0)
    dgate_ref[...] = jnp.concatenate(gates, axis=0)


def weight_kernel(starts, place_ref, *refs):
    x_refs, right_ref, out_ref = refs[: len(starts) - 1], refs[len(starts) - 1], refs[-1]
    step = pl.program_id(0)
    for ref, first, last in zip(x_refs, starts, starts[1:]):

        @pl.when((step >= first) & (step < last))
        def _():
            left = [ref[j, 0] for j in range(ref.shape[0])]
            out_ref[...] = dot(join(left, 1), right_ref[...], NN).astype(out_ref.dtype)


def weight_grad(plain, rest, right, where, blocks, before):
    shards, length = (rest[0] if plain is None else plain).shape[0 :: 2 if plain is None else 3]
    bands = lax.axis_size("head")
    cut = 0 if plain is None else plain.shape[2]
    left_over = rest[0].shape[1] if rest else 0
    block = 1024
    while cut % block or left_over % block or shards * block * length * 4 * (len(rest) + 1) > 2**25:
        block = block // 2
    per, more = cut // block, left_over // block
    total = per + more
    arrays, starts, specs = [], [0], []

    def add(x, steps):
        begin = starts[-1]
        arrays.append(x)
        starts.append(begin + steps)
        inner = x.shape[2] // block

        def index(t, p):
            at = jnp.clip(t - begin, 0, steps - 1)
            return (0, at // inner, at % inner, 0)

        specs.append(pl.BlockSpec((shards, 1, block, length), index))

    if cut:
        add(plain, bands * per)
    for x in rest:
        add(x[:, None], more)

    def out_index(t, p):
        place = (t // max(per, 1)) * total + t % max(per, 1)
        for r in range(len(rest)):
            at = t - bands * per - r * more
            band = (p[0] + bands - r) % bands
            place = jnp.where(at >= 0, band * total + per + at, place)
        return (place, p[1])

    extra = [] if before is None else [before]
    return pl.pallas_call(
        partial(weight_kernel, starts),
        grid_spec=pltpu.PrefetchScalarGridSpec(
            num_scalar_prefetch=1,
            grid=(starts[-1],),
            in_specs=specs
            + [pl.BlockSpec(right.shape, lambda t, p: (0, 0))]
            + [pl.BlockSpec(memory_space=pl.ANY)] * len(extra),
            out_specs=pl.BlockSpec((block, right.shape[1]), out_index),
        ),
        out_shape=jax.ShapeDtypeStruct((bands * total * block, right.shape[1] * blocks), bf16),
        input_output_aliases={len(arrays) + 2: 0} if extra else {},
        compiler_params=pltpu.CompilerParams(vmem_limit_bytes=VMEM_LIMIT),
        cost_estimate=pl.CostEstimate(flops=10**10, bytes_accessed=0, transcendentals=0),
    )(where, *arrays, right, *extra)


def whole_call(kernel, outs, scratch=(), flops=0, scalars=0):
    specs = {}
    if scalars:
        vmem = pl.BlockSpec(memory_space=pltpu.VMEM)
        specs = dict(in_specs=[pl.BlockSpec(memory_space=pltpu.SMEM)] + [vmem] * scalars)
    return pl.pallas_call(
        kernel,
        **specs,
        out_shape=[jax.ShapeDtypeStruct(s, d) for s, d in outs],
        scratch_shapes=[pltpu.VMEM(s, d) for s, d in scratch],
        compiler_params=pltpu.CompilerParams(vmem_limit_bytes=VMEM_LIMIT),
        cost_estimate=pl.CostEstimate(flops=int(flops), bytes_accessed=0, transcendentals=0),
    )


def shards(layer_input, query_rows, key_matrix_rows, value_rows, beta_rows, log_gate, grad_out):
    length, heads = beta_rows.shape
    width = query_rows.shape[1] // heads
    seq = lax.axis_size("seq")
    halves = lax.axis_size("head")
    groups = seq // heads
    count = heads
    members = [[g * heads + i for i in range(heads)] for g in range(groups)]
    far = list(range(4, seq, 4))
    beyond = [m for m in far if m not in (4, 8)]
    me = lax.axis_index("seq").astype(jnp.int32)
    core = lax.axis_index("head").astype(jnp.int32)
    place = jnp.stack([me // heads, jnp.int32(groups)])

    feats = layer_input.shape[1]
    cut = feats * PLAIN // 8
    sizes = [size for size in (cut, feats - cut) if size]
    turned = whole_call(turn_kernel, [((size, length), bf16) for size in sizes])(layer_input)
    plain = None
    if cut:
        plain = lax.all_gather(turned[0], ("seq", "head"), axis=0).reshape(seq, halves, cut, length)
    got = {0: turned[-1]}
    for m in beyond + [1, 2]:
        got[m] = swap(got[0], m)

    slabs = pack([query_rows, key_matrix_rows, value_rows, grad_out], beta_rows.T, log_gate.T)
    slabs = lax.all_to_all(slabs, "seq", 0, 0, axis_index_groups=members, tiled=True)
    for m in far[:1]:
        got[m] = swap(got[0], m)

    square = (width, width)
    maps, aux, ends = whole_call(
        first_kernel,
        [((count, 3) + square, f32), ((count, 4, length, width), f32), ((4,) + square, f32)],
        [((count, length, length), f32), ((count, length, length), f32)],
        9e9,
        1,
    )(place, slabs)

    got = after(got, list(got), ends)
    corner(got, 0)
    if 12 in got:
        got[8] = swap(got[12], 4)
    for m in beyond:
        sides(got, m)

    up = [(s, s + heads) for s in range(seq - heads)]
    down = [(s + heads, s) for s in range(seq - heads)]
    if groups == 2:
        start = finish = lax.ppermute(ends[3], "seq", up + down)
    else:
        start = lax.ppermute(ends[0], "seq", up)
        finish = lax.ppermute(ends[1], "seq", down)
        for _ in range(groups - 2):
            start = lax.ppermute(
                jnp.matmul(ends[2], start, precision=lax.Precision.HIGHEST) + ends[0], "seq", up
            )
            finish = lax.ppermute(
                jnp.matmul(finish, ends[2], precision=lax.Precision.HIGHEST) + ends[1], "seq", down
            )

    if groups == 2:
        start, got = tied(start, got, [3, 4, 8, 13, 14])
        finish = start
    for m in far[:2]:
        sides(got, m)
    for m in beyond:
        corner(got, m)

    dv, grads = whole_call(
        second_kernel,
        [((count, length, width), bf16), ((count, 2 * length + PAD, width), bf16)],
        [((count,) + square, f32), ((count,) + square, f32)],
        7e9,
        5,
    )(place, slabs, maps, aux, start, finish)

    dv, got = tied(dv, got, [m for m in (9, 10) if m in got])
    sent = {0: dv}
    for m in beyond[1:] + far[1:2] + [1, 2]:
        sent[m] = swap(dv, m)
    for m in far[:2]:
        corner(got, m)
    sent, got = lax.optimization_barrier((sent, got))
    for m in far[1:2]:
        sides(sent, m)
    for m in far[:1]:
        sent[m] = swap(dv, m)
    if 8 in sent:
        sent[12] = swap(sent[8], 4)
    sent[3] = swap(sent[2], 1)
    (own,) = arranged(stack_kernel, got, me, [(seq,) + got[0].shape])
    own, sent = tied(own, sent, list(sent))
    rest = [own]
    for r in range(1, halves):
        rest.append(lax.ppermute(own, "head", [(i, (i + r) % halves) for i in range(halves)]))
    for m in far[1:2]:
        sent[m | 3] = swap(sent[m | 1], 2)
    for m in far[:1] + beyond:
        sides(sent, m)

    sent = after(sent, [m for m in sent if m % 8 > 3], sent[11 if 8 in sent else 3])
    for m in far[:1] + beyond:
        corner(sent, m)

    rows = (length, heads * width)
    (dvo,) = arranged(rows_kernel, {m: sent[m] for m in range(heads)}, me, [rows])
    weight = None
    part = max(heads // 2, 1)
    for bit in sorted({0, part % heads}):
        some = {m: sent[m] for m in range(seq) if m & part == bit or heads == 1}
        if weight is not None:
            some = after(some, list(some), weight)
        (right,) = arranged(partial(place_kernel, list(some), heads), some, me, [(groups, count, length, part * width)])
        where = jnp.stack([core, (me % heads ^ bit) // part])
        weight = weight_grad(plain, rest, right.reshape(seq * length, part * width), where, heads // part, weight)

    back = lax.all_to_all(grads, "seq", 0, 0, axis_index_groups=members, tiled=True)
    rows = (length, heads * width)
    back = lax.optimization_barrier((back, weight))[0]
    dq, dk, dbeta, dgate = whole_call(
        unpack_kernel, [(rows, bf16), (rows, bf16), ((heads, length), f32), ((heads, length), f32)]
    )(back)
    return dq, dk, dvo, dbeta.T, dgate.T, weight


def solution(mesh):
    row = P("seq", "head")
    return jax.shard_map(
        shards, mesh=mesh, in_specs=(row,) * 7, out_specs=(row,) * 5 + (P(None, "head"),), check_vma=False
    )
```

```python
from functools import partial

import jax
import jax.numpy as jnp
from jax import lax
from jax.experimental import pallas as pl
from jax.experimental.pallas import tpu as pltpu
from jax.sharding import PartitionSpec as P

f32 = jnp.float32
bf16 = jnp.bfloat16
PAD = 16
PLAIN = 0
VMEM_MOST = 60 * 1024 * 1024
VMEM_LIMIT = 48 * 1024 * 1024

NN = (((1,), (0,)), ((), ()))
NT = (((1,), (1,)), ((), ()))
TN = (((0,), (0,)), ((), ()))


def dot(a, b, dims):
    return lax.dot_general(a, b, dims, preferred_element_type=f32)


def split(x):
    hi = x.astype(bf16)
    return hi, (x - hi.astype(f32)).astype(bf16)


def join(parts, axis):
    return jnp.concatenate(parts, axis=axis)


def mm(a, b, dims):
    (ca,), (cb,) = dims[0]
    if isinstance(a, tuple) and isinstance(b, tuple):
        return dot(join([a[0], a[1], a[0]], ca), join([b[0], b[0], b[1]], cb), dims)
    if isinstance(a, tuple):
        return dot(join([a[0], a[1]], ca), join([b, b], cb), dims)
    if isinstance(b, tuple):
        return dot(join([a, a], ca), join([b[0], b[1]], cb), dims)
    return dot(a, b, dims)


def thirds(x):
    one = x.astype(bf16)
    rest = x - one.astype(f32)
    two = rest.astype(bf16)
    return one, two, (rest - two.astype(f32)).astype(bf16)


def pack_scalars(first, second):
    pieces = [p.astype(f32) for p in thirds(first) + thirds(second)]
    rows, width = first.shape
    out = []
    for r in range(rows):
        lines = [p[r : r + 1] for p in pieces] + [jnp.zeros((PAD - 6, width), f32)]
        out.append(jnp.concatenate(lines, axis=0).astype(bf16))
    return out


def unpack_scalars(tile):
    t = tile.astype(f32)
    return t[0:1] + t[1:2] + t[2:3], t[3:4] + t[4:5] + t[5:6]


def iotas(size):
    return (
        lax.broadcasted_iota(jnp.int32, (size, size), 0),
        lax.broadcasted_iota(jnp.int32, (size, size), 1),
    )


def turn_kernel(x_ref, *out_refs):
    first = 0
    for out_ref in out_refs:
        here = out_ref.shape[0]
        out_ref[...] = jnp.transpose(x_ref[:, pl.ds(first, here)])
        first += here


def pack_kernel(q_ref, k_ref, v_ref, g_ref, beta_ref, gate_ref, out_ref, sems):
    heads, length = beta_ref.shape
    width = q_ref.shape[1] // heads
    copies = []
    for h in range(heads):
        for place, ref in enumerate((q_ref, k_ref, v_ref, g_ref)):
            copies.append(
                pltpu.make_async_copy(
                    ref.at[:, pl.ds(h * width, width)],
                    out_ref.at[h, pl.ds(place * length, length), :],
                    sems.at[h, place],
                )
            )
            copies[-1].start()
    for h, lines in enumerate(pack_scalars(beta_ref[...], gate_ref[...])):
        out_ref[h, pl.ds(4 * length, PAD), :] = lines
    for copy in copies:
        copy.wait()


def pack(arrays, beta, gate):
    heads, length = beta.shape
    width = arrays[0].shape[1] // heads
    return pl.pallas_call(
        pack_kernel,
        in_specs=[pl.BlockSpec(memory_space=pl.ANY)] * 4 + [pl.BlockSpec(memory_space=pltpu.VMEM)] * 2,
        out_specs=pl.BlockSpec(memory_space=pltpu.VMEM),
        out_shape=jax.ShapeDtypeStruct((heads, 4 * length + PAD, width), bf16),
        scratch_shapes=[pltpu.SemaphoreType.DMA((heads, 4))],
        compiler_params=pltpu.CompilerParams(vmem_limit_bytes=VMEM_MOST),
    )(*arrays, beta, gate)


def scalars_of(slab_ref, count, length):
    betas, gates = [], []
    for c in range(count):
        b, g = unpack_scalars(slab_ref[c, pl.ds(4 * length, PAD), :])
        betas.append(b)
        gates.append(g)
    beta = jnp.concatenate(betas, axis=0)
    gate = jnp.concatenate(gates, axis=0)
    line, col = iotas(length)
    upper = (line <= col).astype(f32)
    running = lax.dot_general(
        gate, upper, NN, precision=lax.Precision.HIGHEST, preferred_element_type=f32
    )
    return running, jnp.transpose(running), jnp.transpose(beta)


def decay_of(run_col, run_row, causal):
    return jnp.where(causal, jnp.exp(jnp.where(causal, run_col - run_row, 0.0)), 0.0)


def first_kernel(chained, place_ref, slab_ref, maps_ref, aux_ref, ends_ref, inv_ref, low_ref):
    count = slab_ref.shape[0]
    width = slab_ref.shape[2]
    length = (slab_ref.shape[1] - PAD) // 4
    running, run_cols, beta_cols = scalars_of(slab_ref, count, length)
    line, col = iotas(length)
    causal = line >= col
    strict = line > col
    eye = (line == col).astype(f32)

    def part(c, place):
        return slab_ref[c, pl.ds(place * length, length), :]

    for c in range(count):
        decay = decay_of(run_cols[:, c : c + 1], running[c : c + 1, :], causal)
        k = part(c, 1)
        low = jnp.where(strict, beta_cols[:, c : c + 1] * decay * dot(k, k, NT), 0.0)
        low_ref[c] = low
        inv_ref[c] = eye - jnp.where((line ^ col) == 1, low, 0.0)
    size = 2
    while size < length:
        mask = ((line // size) ^ (col // size)) == 1
        for c in range(count):
            inv = split(inv_ref[c])
            side = split(jnp.where(mask, low_ref[c], 0.0))
            mid = split(mm(side, inv, NN))
            inv_ref[c] = inv_ref[c] - mm(inv, mid, NN)
        size = size * 2

    for c in range(count):
        run_col = run_cols[:, c : c + 1]
        beta = beta_cols[:, c : c + 1]
        grow = jnp.exp(run_col)
        last = running[c : c + 1, length - 1 : length]
        tail = jnp.exp(last - run_col)
        decay = decay_of(run_col, running[c : c + 1, :], causal)
        q, k, v, g = (part(c, i) for i in range(4))
        qf, kf, vf, gf = (a.astype(f32) for a in (q, k, v, g))
        inv = split(inv_ref[c])
        pairs = split(decay * dot(q, k, NT))
        both = mm(inv, split(join([(beta * grow) * kf, beta * vf], 1)), NN)
        aux_ref[c, 0] = both[:, :width]
        aux_ref[c, 1] = both[:, width:]
        moved = mm(k, split(tail * both), TN)
        eye_d = (
            lax.broadcasted_iota(jnp.int32, (width, width), 0)
            == lax.broadcasted_iota(jnp.int32, (width, width), 1)
        ).astype(f32)
        maps_ref[c, 0] = jnp.exp(last) * eye_d - moved[:, :width]
        maps_ref[c, 1] = moved[:, width:]
        back = mm(inv, split(join([mm(pairs, g, TN), tail * kf], 1)), TN)
        aux_ref[c, 2] = back[:, :width]
        aux_ref[c, 3] = back[:, width:]
        maps_ref[c, 2] = mm(g, split(grow * qf), TN) - mm(split((beta * grow) * back[:, :width]), k, TN)

    state = maps_ref[0, 1]
    adjoint = maps_ref[count - 1, 2]
    total = maps_ref[0, 0]
    for c in range(1, count):
        trans = split(maps_ref[c, 0])
        state = mm(trans, split(state), NN) + maps_ref[c, 1]
        if chained:
            total = mm(trans, split(total), NN)
        r = count - 1 - c
        adjoint = mm(split(adjoint), split(maps_ref[r, 0]), NN) + maps_ref[r, 2]
    ends_ref[0] = state
    ends_ref[1] = adjoint
    ends_ref[2] = total
    ends_ref[3] = jnp.where(place_ref[0] == 0, state, adjoint)


def second_kernel(place_ref, slab_ref, maps_ref, aux_ref, start_ref, finish_ref, dv_ref, out_ref, state_ref, adj_ref):
    count = slab_ref.shape[0]
    width = slab_ref.shape[2]
    length = (slab_ref.shape[1] - PAD) // 4
    running, run_cols, beta_cols = scalars_of(slab_ref, count, length)
    line, col = iotas(length)
    causal = line >= col
    strict = line > col

    state_ref[0] = jnp.where(place_ref[0] == 0, 0.0, start_ref[...])
    adj_ref[count - 1] = jnp.where(place_ref[0] == place_ref[1] - 1, 0.0, finish_ref[...])
    for c in range(1, count):
        state_ref[c] = mm(split(maps_ref[c - 1, 0]), split(state_ref[c - 1]), NN) + maps_ref[c - 1, 1]
        r = count - 1 - c
        adj_ref[r] = mm(split(adj_ref[r + 1]), split(maps_ref[r + 1, 0]), NN) + maps_ref[r + 1, 2]

    grad_beta, grad_run, consts = [], [], []
    for c in range(count):
        run_col = run_cols[:, c : c + 1]
        beta = beta_cols[:, c : c + 1]
        grow = jnp.exp(run_col)
        last = running[c : c + 1, length - 1 : length]
        tail = jnp.exp(last - run_col)
        decay = decay_of(run_col, running[c : c + 1, :], causal)
        q, k, v, g = (slab_ref[c, pl.ds(i * length, length), :] for i in range(4))
        qf, kf, vf = (a.astype(f32) for a in (q, k, v))
        state = state_ref[c]
        adj = adj_ref[c]
        state_s, adj_s = split(state), split(adj)
        update = aux_ref[c, 1] - mm(split(aux_ref[c, 0]), state_s, NN)
        update_s = split(update)
        d_rhs = aux_ref[c, 2] + mm(split(aux_ref[c, 3]), adj_s, NT)
        d_rhs_s = split(d_rhs)
        d_pair = decay * mm(g, update_s, NT)
        d_low = jnp.where(strict, -decay * mm(d_rhs_s, update_s, NT), 0.0)
        dq = grow * mm(g, state_s, NT) + mm(split(d_pair), k, NN)
        row = mm(split(d_low), k, NN) - grow * mm(d_rhs_s, state_s, NT)
        dk_row = beta * row
        wrote = tail * mm(update_s, adj_s, NN)
        dk_col = wrote + mm(split(join([d_pair, beta * d_low], 0)), join([q, k], 0), TN)
        dv_ref[c] = (beta * d_rhs).astype(bf16)
        out_ref[c, pl.ds(0, length), :] = dq.astype(bf16)
        out_ref[c, pl.ds(length, length), :] = (dk_row + dk_col).astype(bf16)
        grad_beta.append(jnp.sum(d_rhs * vf + kf * row, axis=1, keepdims=True))
        grad_run.append(jnp.sum(qf * dq + kf * (dk_row - dk_col), axis=1, keepdims=True))
        carry = jnp.exp(last) * jnp.sum(state * jnp.transpose(adj)) + jnp.sum(kf * wrote)
        consts.append(carry)
    db = jnp.concatenate(grad_beta, axis=1)
    dr = jnp.concatenate(grad_run, axis=1)
    upper = (line <= col).astype(f32)
    dg = lax.dot_general(
        upper, dr, NN, precision=lax.Precision.HIGHEST, preferred_element_type=f32
    ) + jnp.concatenate(consts, axis=1)
    packed = pack_scalars(jnp.transpose(db), jnp.transpose(dg))
    for c in range(count):
        out_ref[c, pl.ds(2 * length, PAD), :] = packed[c]


def swap(x, mask):
    return lax.ppermute(x, "seq", [(i, i ^ mask) for i in range(lax.axis_size("seq"))])


def corner(got, m):
    got[m | 3] = swap(got[m | 2], 1) if m == 12 else swap(got[m | 1], 2)


def sides(got, m):
    if m == 4:
        got[5], got[6] = swap(got[1], 4), swap(got[2], 4)
    else:
        got[m | 1], got[m | 2] = swap(got[m], 1), swap(got[m], 2)


def after(got, masks, *others):
    some = {m: got[m] for m in masks}
    return {**got, **lax.optimization_barrier((some,) + others)[0]}


def tied(x, got, masks):
    x, some = lax.optimization_barrier((x, {m: got[m] for m in masks if m in got}))
    return x, {**got, **some}


def stack_kernel(me_ref, *refs):
    parts, out_ref, sems = refs[:-2], refs[-2], refs[-1]
    copies = []
    for mask, part in enumerate(parts):
        copies.append(pltpu.make_async_copy(part, out_ref.at[me_ref[0] ^ mask], sems.at[mask]))
        copies[-1].start()
    for copy in copies:
        copy.wait()


def place_kernel(masks, all_heads, me_ref, *refs):
    parts, all_ref, sems = refs[:-2], refs[-2], refs[-1]
    width = parts[0].shape[2]
    heads = all_ref.shape[3] // width
    copies = []
    for i, (mask, part) in enumerate(zip(masks, parts)):
        source = me_ref[0] ^ mask
        lanes = pl.ds(pl.multiple_of(source % heads * width, width), width)
        copies.append(pltpu.make_async_copy(part, all_ref.at[source // all_heads, :, :, lanes], sems.at[i]))
        copies[-1].start()
    for copy in copies:
        copy.wait()


def rows_kernel(me_ref, *refs):
    parts, rows_ref, sems = refs[:-2], refs[-2], refs[-1]
    heads, width = len(parts), parts[0].shape[2]
    me = me_ref[0]
    copies = []
    for mask, part in enumerate(parts):
        lanes = pl.ds(pl.multiple_of((me ^ mask) % heads * width, width), width)
        copies.append(pltpu.make_async_copy(part.at[me % heads], rows_ref.at[:, lanes], sems.at[mask]))
        copies[-1].start()
    for copy in copies:
        copy.wait()


def arranged(kernel, got, me, outs):
    parts = [got[m] for m in sorted(got)]
    vmem = pl.BlockSpec(memory_space=pltpu.VMEM)
    return pl.pallas_call(
        kernel,
        in_specs=[pl.BlockSpec(memory_space=pltpu.SMEM)] + [pl.BlockSpec(memory_space=pl.ANY)] * len(parts),
        out_specs=[vmem] * len(outs),
        out_shape=[jax.ShapeDtypeStruct(o, bf16) for o in outs],
        scratch_shapes=[pltpu.SemaphoreType.DMA((len(parts),))],
        compiler_params=pltpu.CompilerParams(vmem_limit_bytes=VMEM_LIMIT),
    )(me.reshape(1), *parts)


def unpack_kernel(back_ref, dq_ref, dk_ref, dbeta_ref, dgate_ref):
    heads = back_ref.shape[0]
    length, width = dq_ref.shape[0], dq_ref.shape[1] // heads
    betas, gates = [], []
    for h in range(heads):
        lanes = pl.ds(h * width, width)
        dq_ref[:, lanes] = back_ref[h, pl.ds(0, length), :]
        dk_ref[:, lanes] = back_ref[h, pl.ds(length, length), :]
        b, g = unpack_scalars(back_ref[h, pl.ds(2 * length, PAD), :])
        betas.append(b)
        gates.append(g)
    dbeta_ref[...] = jnp.concatenate(betas, axis=0)
    dgate_ref[...] = jnp.concatenate(gates, axis=0)


def weight_kernel(starts, place_ref, *refs):
    x_refs, right_ref, out_ref = refs[: len(starts) - 1], refs[len(starts) - 1], refs[-1]
    step = pl.program_id(0)
    for ref, first, last in zip(x_refs, starts, starts[1:]):

        @pl.when((step >= first) & (step < last))
        def _():
            left = [ref[j, 0] for j in range(ref.shape[0])]
            out_ref[...] = dot(join(left, 1), right_ref[...], NN).astype(out_ref.dtype)


def weight_grad(plain, rest, right, where, blocks, before):
    shards, length = (rest[0] if plain is None else plain).shape[0 :: 2 if plain is None else 3]
    bands = lax.axis_size("head")
    cut = 0 if plain is None else plain.shape[2]
    left_over = rest[0].shape[1] if rest else 0
    block = 1024
    while cut % block or left_over % block or shards * block * length * 4 * (len(rest) + 1) > 2**25:
        block = block // 2
    per, more = cut // block, left_over // block
    total = per + more
    arrays, starts, specs = [], [0], []

    def add(x, steps):
        begin = starts[-1]
        arrays.append(x)
        starts.append(begin + steps)
        inner = x.shape[2] // block

        def index(t, p):
            at = jnp.clip(t - begin, 0, steps - 1)
            return (0, at // inner, at % inner, 0)

        specs.append(pl.BlockSpec((shards, 1, block, length), index))

    if cut:
        add(plain, bands * per)
    for x in rest:
        add(x[:, None], more)

    def out_index(t, p):
        place = (t // max(per, 1)) * total + t % max(per, 1)
        for r in range(len(rest)):
            at = t - bands * per - r * more
            band = (p[0] + bands - r) % bands
            place = jnp.where(at >= 0, band * total + per + at, place)
        return (place, p[1])

    extra = [] if before is None else [before]
    return pl.pallas_call(
        partial(weight_kernel, starts),
        grid_spec=pltpu.PrefetchScalarGridSpec(
            num_scalar_prefetch=1,
            grid=(starts[-1],),
            in_specs=specs
            + [pl.BlockSpec(right.shape, lambda t, p: (0, 0))]
            + [pl.BlockSpec(memory_space=pl.ANY)] * len(extra),
            out_specs=pl.BlockSpec((block, right.shape[1]), out_index),
        ),
        out_shape=jax.ShapeDtypeStruct((bands * total * block, right.shape[1] * blocks), bf16),
        input_output_aliases={len(arrays) + 2: 0} if extra else {},
        compiler_params=pltpu.CompilerParams(vmem_limit_bytes=VMEM_LIMIT),
        cost_estimate=pl.CostEstimate(flops=10**10, bytes_accessed=0, transcendentals=0),
    )(where, *arrays, right, *extra)


def whole_call(kernel, outs, scratch=(), flops=0, scalars=0):
    specs = {}
    if scalars:
        vmem = pl.BlockSpec(memory_space=pltpu.VMEM)
        specs = dict(in_specs=[pl.BlockSpec(memory_space=pltpu.SMEM)] + [vmem] * scalars)
    return pl.pallas_call(
        kernel,
        **specs,
        out_shape=[jax.ShapeDtypeStruct(s, d) for s, d in outs],
        scratch_shapes=[pltpu.VMEM(s, d) for s, d in scratch],
        compiler_params=pltpu.CompilerParams(vmem_limit_bytes=VMEM_LIMIT),
        cost_estimate=pl.CostEstimate(flops=int(flops), bytes_accessed=0, transcendentals=0),
    )


def shards(layer_input, query_rows, key_matrix_rows, value_rows, beta_rows, log_gate, grad_out):
    length, heads = beta_rows.shape
    width = query_rows.shape[1] // heads
    seq = lax.axis_size("seq")
    halves = lax.axis_size("head")
    groups = seq // heads
    count = heads
    members = [[g * heads + i for i in range(heads)] for g in range(groups)]
    far = list(range(4, seq, 4))
    beyond = [m for m in far if m not in (4, 8)]
    me = lax.axis_index("seq").astype(jnp.int32)
    core = lax.axis_index("head").astype(jnp.int32)
    place = jnp.stack([me // heads, jnp.int32(groups)])

    feats = layer_input.shape[1]
    cut = feats * PLAIN // 8
    sizes = [size for size in (cut, feats - cut) if size]
    turned = whole_call(turn_kernel, [((size, length), bf16) for size in sizes])(layer_input)
    plain = None
    if cut:
        plain = lax.all_gather(turned[0], ("seq", "head"), axis=0).reshape(seq, halves, cut, length)
    got = {0: turned[-1]}
    for m in beyond + [1, 2]:
        got[m] = swap(got[0], m)

    slabs = pack([query_rows, key_matrix_rows, value_rows, grad_out], beta_rows.T, log_gate.T)
    slabs = lax.all_to_all(slabs, "seq", 0, 0, axis_index_groups=members, tiled=True)
    for m in far[:1]:
        got[m] = swap(got[0], m)

    square = (width, width)
    maps, aux, ends = whole_call(
        partial(first_kernel, groups > 2),
        [((count, 3) + square, f32), ((count, 4, length, width), f32), ((4,) + square, f32)],
        [((count, length, length), f32), ((count, length, length), f32)],
        9e9,
        1,
    )(place, slabs)

    got = after(got, list(got), ends)
    corner(got, 0)
    if 12 in got:
        got[8] = swap(got[12], 4)
    for m in beyond:
        sides(got, m)

    up = [(s, s + heads) for s in range(seq - heads)]
    down = [(s + heads, s) for s in range(seq - heads)]
    if groups == 2:
        start = finish = lax.ppermute(ends[3], "seq", up + down)
    else:
        start = lax.ppermute(ends[0], "seq", up)
        finish = lax.ppermute(ends[1], "seq", down)
        for _ in range(groups - 2):
            start = lax.ppermute(
                jnp.matmul(ends[2], start, precision=lax.Precision.HIGHEST) + ends[0], "seq", up
            )
            finish = lax.ppermute(
                jnp.matmul(finish, ends[2], precision=lax.Precision.HIGHEST) + ends[1], "seq", down
            )

    if groups == 2:
        start, got = tied(start, got, [3, 4, 8, 13, 14])
        finish = start
    for m in far[:2]:
        sides(got, m)
    for m in beyond:
        corner(got, m)

    dv, grads = whole_call(
        second_kernel,
        [((count, length, width), bf16), ((count, 2 * length + PAD, width), bf16)],
        [((count,) + square, f32), ((count,) + square, f32)],
        7e9,
        5,
    )(place, slabs, maps, aux, start, finish)

    dv, got = tied(dv, got, [m for m in (9, 10) if m in got])
    sent = {0: dv}
    for m in beyond[1:] + far[1:2] + [1, 2]:
        sent[m] = swap(dv, m)
    for m in far[:2]:
        corner(got, m)
    sent, got = lax.optimization_barrier((sent, got))
    for m in far[1:2]:
        sides(sent, m)
    for m in far[:1]:
        sent[m] = swap(dv, m)
    if 8 in sent:
        sent[12] = swap(sent[8], 4)
    sent[3] = swap(sent[2], 1)
    (own,) = arranged(stack_kernel, got, me, [(seq,) + got[0].shape])
    own, sent = tied(own, sent, list(sent))
    rest = [own]
    for r in range(1, halves):
        rest.append(lax.ppermute(own, "head", [(i, (i + r) % halves) for i in range(halves)]))
    for m in far[1:2]:
        sent[m | 3] = swap(sent[m | 1], 2)
    for m in far[:1] + beyond:
        sides(sent, m)

    sent = after(sent, [m for m in sent if m % 8 > 3], sent[11 if 8 in sent else 3])
    for m in far[:1] + beyond:
        corner(sent, m)

    rows = (length, heads * width)
    (dvo,) = arranged(rows_kernel, {m: sent[m] for m in range(heads)}, me, [rows])
    weight = None
    part = max(heads // 2, 1)
    for bit in sorted({0, part % heads}):
        some = {m: sent[m] for m in range(seq) if m & part == bit or heads == 1}
        if weight is not None:
            some = after(some, list(some), weight)
        (right,) = arranged(partial(place_kernel, list(some), heads), some, me, [(groups, count, length, part * width)])
        where = jnp.stack([core, (me % heads ^ bit) // part])
        weight = weight_grad(plain, rest, right.reshape(seq * length, part * width), where, heads // part, weight)

    back = lax.all_to_all(grads, "seq", 0, 0, axis_index_groups=members, tiled=True)
    rows = (length, heads * width)
    back = lax.optimization_barrier((back, weight))[0]
    dq, dk, dbeta, dgate = whole_call(
        unpack_kernel, [(rows, bf16), (rows, bf16), ((heads, length), f32), ((heads, length), f32)]
    )(back)
    return dq, dk, dvo, dbeta.T, dgate.T, weight


def solution(mesh):
    row = P("seq", "head")
    return jax.shard_map(
        shards, mesh=mesh, in_specs=(row,) * 7, out_specs=(row,) * 5 + (P(None, "head"),), check_vma=False
    )
```
